32 devices in a mesh: row: 8 (over y, x, core), col: 4 (over z).
Axes of the slice: x: 2, y: 2, z: 4, core: 2. Of those that a mesh axis runs over, the one named last changes fastest.
Arguments:
- tokens: bfloat16 [32768, 768], P(('row', 'col')), may hold values from -6 to 6
- gate_prob: bfloat16 [32768], P(('row', 'col')), may hold values from 0.19921875 to 1
- expert_id: int32 [32768], P(('row', 'col')), may hold values from 0 to 63, as said below
- dest_row: int32 [32768], P(('row', 'col')), may hold values from 0 to 32767, as said below
- ff_gain: float32 [768], replicated, may hold values from 0.5 to 1.5
- expert_in: bfloat16 [64, 768, 3072], P(('row', 'col')), may hold values from -0.21875 to 0.21875
- expert_out: bfloat16 [64, 3072, 768], P(('row', 'col')), may hold values from -0.109375 to 0.109375
- attn_gain: float32 [768], replicated, may hold values from 0.5 to 1.5
- qkv_weight: bfloat16 [768, 2304], P(None, 'row'), may hold values from -8 to 8
- mix_weight: bfloat16 [768, 768], P(None, 'row'), may hold values from -1.75 to 1.75
Outputs:
- moe_out: bfloat16 [32768, 768], P(('row', 'col'))
- attn_branch: bfloat16 [32768, 768], P(('row', 'col'))
The draws below stay inside these ranges and needn't reach their ends.
Inputs may be any that keep to these rules, and one draw needn't show every extreme that they name: `expert_id`: expert e's weights are held by device e // 2 (its local index e % 2). Each expert is named by at most 768 tokens in all, and some expert by exactly 768. Within the rows of one device no expert is named more than 26 times, and some device names some expert exactly 26 times. The rows of one device name the experts of any one device, together, exactly 32 times. `dest_row`: A permutation of all rows. Owner device o holds rows o * 1024 to (o + 1) * 1024 - 1; the rows of every device go to every owner exactly 32 times, and of the rows whose experts one device holds, exactly 32 go to every owner.
All inputs are finite; a program needn't handle non-finite values.
Results may differ from the reference program's by a relative error of at most 0.012.
Values may be sent and summed in bfloat16 or wider, within the bound.
A program may use at most 128 MiB of HBM per device.

```python
import math
import jax
import jax.numpy as jnp
from jax import lax

D = 768
FF = 3072
HEADS = 12
HEAD_DIM = 64
SEQ = 512
TOK_DEV = 1024
EXPERTS = 64
TOKENS = 32768
CAP = 768


def draw_routing(key):
    devices = TOKENS // TOK_DEV
    unit = CAP // 6 // devices
    per_owner = TOK_DEV // devices
    keys = jax.random.split(jax.random.fold_in(key, 5), 5)
    ranking = jax.random.permutation(keys[0], devices).astype(jnp.int32)
    flavour = ranking % 2
    flipped = ranking // 2 % 2
    sign_first = (1 - 2 * (ranking // 4 % 2)).astype(jnp.int32)
    higher = jnp.where(flavour == 0, 6, 5).astype(jnp.int32)
    level_first = jnp.where(flipped == 0, higher, 8 - higher).astype(jnp.int32)
    levels = jnp.stack([level_first, 8 - level_first], axis=1).reshape(EXPERTS)
    expert_sign = jnp.stack([sign_first, -sign_first], axis=1).reshape(EXPERTS)
    source_rank = jax.random.permutation(keys[1], devices).astype(jnp.int32)
    source_sign = jnp.where(source_rank < devices // 2, 1, -1).astype(jnp.int32)
    counts = unit * levels[None, :] + 2 * source_sign[:, None] * expert_sign[None, :]
    bounds = jnp.cumsum(counts, axis=1).astype(jnp.int32)
    positions = jnp.arange(TOK_DEV, dtype=jnp.int32)

    def expand(bound_row):
        return jnp.sum((bound_row[None, :] <= positions[:, None]).astype(jnp.int32), axis=1)
    sorted_labels = lax.map(expand, bounds).astype(jnp.int32)
    shifting = jax.random.permutation(keys[2], devices).astype(jnp.int32)
    owners = (positions[None, :] + shifting[:, None]) % devices
    sources = jnp.arange(devices, dtype=jnp.int32)
    arrival = sources[:, None] * per_owner + positions[None, :] // devices
    owner_perm = jax.vmap(lambda row_key: jax.random.permutation(row_key, TOK_DEV))(jax.random.split(keys[3], devices)).astype(jnp.int32)
    destination = owners * TOK_DEV + owner_perm[owners, arrival]
    token_perm = jax.vmap(lambda row_key: jax.random.permutation(row_key, TOK_DEV))(jax.random.split(keys[4], devices)).astype(jnp.int32)
    labels = jnp.zeros((devices, TOK_DEV), jnp.int32).at[sources[:, None], token_perm].set(sorted_labels)
    placed = jnp.zeros((devices, TOK_DEV), jnp.int32).at[sources[:, None], token_perm].set(destination)
    return (labels.reshape(TOKENS).astype(jnp.int32), placed.reshape(TOKENS).astype(jnp.int32))


def draw_expert_id(key, part):
    labels, placed = draw_routing(key)
    return labels


def draw_dest_row(key, part):
    labels, placed = draw_routing(key)
    return placed


def draw_qkv_weight(key, part):
    key = jax.random.fold_in(key, 37)
    first_key = jax.random.fold_in(key, 0)
    second_key = jax.random.fold_in(key, 1)
    fourth_key = jax.random.fold_in(key, 3)
    root = math.sqrt(D)
    value_part = jnp.clip(jax.random.normal(fourth_key, (D, D), jnp.float32), -4.0, 4.0) / root
    query_part = jnp.clip(jax.random.normal(first_key, (D, D), jnp.float32), -4.0, 4.0) / root
    key_part = jnp.clip(jax.random.normal(second_key, (D, D), jnp.float32), -4.0, 4.0) / root
    return jnp.concatenate([query_part, key_part, value_part], axis=1).astype(jnp.bfloat16)


def steps_of(rng, dims, shards, low, high):
    def one(axis_at, shards_of):
        steps = jax.random.uniform(jax.random.fold_in(jax.random.fold_in(rng, 6), axis_at), (shards_of,), jnp.float32, low / len(shards), high / len(shards))
        return jnp.repeat(jnp.exp(steps), dims[axis_at] // shards_of).reshape((-1,) + (1,) * (len(dims) - axis_at - 1))

    gain = one(*shards[0])
    for cut in shards[1:]:
        gain = gain * one(*cut)
    return gain


def gaussian(own_key, dims, spread, limit, pieces=(), kind=jnp.bfloat16):
    array = spread * jax.random.normal(own_key, dims, jnp.float32)
    if pieces:
        array = array * steps_of(own_key, dims, pieces, -0.22, 0.18)
    return jnp.clip(array, -limit, limit).astype(kind)


def setup_inputs(seed: int = 0) -> dict:
    splits = jax.random.split(jax.random.key(seed), 11)
    return {
        "tokens": gaussian(splits[0], (TOKENS, D), 1.0, 6.0, ((0, 32),)),
        "gate_prob": jnp.clip(jnp.exp(math.log(1.0) - 1.6133518 * jax.random.uniform(splits[1], (TOKENS,), jnp.float32) ** steps_of(splits[1], (TOKENS,), ((0, 32),), -0.2, 0.2)), 0.19921875, 1.0).astype(jnp.bfloat16),
        "expert_id": draw_expert_id(jax.random.fold_in(splits[10], 71), 0),
        "dest_row": draw_dest_row(jax.random.fold_in(splits[10], 71), 0),
        "ff_gain": jnp.clip(jax.random.uniform(splits[4], (D,), jnp.float32, 0.5, 1.5), 0.5, 1.5),
        "expert_in": gaussian(splits[5], (EXPERTS, D, FF), D ** -0.5, 0.21875, ((0, 32),)),
        "expert_out": gaussian(splits[6], (EXPERTS, FF, D), FF ** -0.5, 0.109375, ((0, 32),)),
        "attn_gain": jnp.clip(jax.random.uniform(splits[7], (D,), jnp.float32, 0.5, 1.5), 0.5, 1.5),
        "qkv_weight": draw_qkv_weight(jax.random.fold_in(splits[10], 71), 0),
        "mix_weight": gaussian(splits[9], (D, D), HEADS ** -0.5, 1.75, ((1, 8),)),
    }


EPSILON = 1e-06

def rms_scale(values, scaling):
    widened = values.astype(jnp.float32)
    power = lax.optimization_barrier(jnp.mean(widened * widened, axis=-1, keepdims=True))
    return (widened * lax.rsqrt(power + EPSILON) * scaling).astype(jnp.bfloat16)

def reference(tokens, gate_prob, expert_id, dest_row, ff_gain, expert_in, expert_out, attn_gain, qkv_weight, mix_weight):
    total = tokens.shape[0]
    normed = rms_scale(tokens, ff_gain)
    per_expert = jnp.zeros((EXPERTS,), jnp.int32).at[expert_id].add(jnp.ones((total,), jnp.int32))
    firsts = jnp.cumsum(per_expert) - per_expert
    sorting = jnp.argsort(expert_id, stable=True).astype(jnp.int32)
    sorted_rank = jnp.arange(total, dtype=jnp.int32) - firsts[expert_id[sorting]]
    within = jnp.zeros((total,), jnp.int32).at[sorting].set(sorted_rank)
    buffers = jnp.zeros((EXPERTS, CAP, D), jnp.bfloat16).at[expert_id, within].set(normed)

    def run_expert(operands):
        rows, first_layer, second_layer = operands
        hidden = jnp.maximum(jnp.dot(rows, first_layer, preferred_element_type=jnp.float32), 0.0).astype(jnp.bfloat16)
        return jnp.dot(hidden, second_layer, preferred_element_type=jnp.float32).astype(jnp.bfloat16)
    results = lax.map(run_expert, (buffers, expert_in, expert_out))
    answer = results[expert_id, within]
    combined = (tokens.astype(jnp.float32) + gate_prob.astype(jnp.float32)[:, None] * answer.astype(jnp.float32)).astype(jnp.bfloat16)
    moe_out = jnp.zeros((total, D), jnp.bfloat16).at[dest_row].set(combined)
    attn_normed = rms_scale(moe_out, attn_gain)
    scale = 1.0 / HEAD_DIM ** 0.5

    def attend(rows):
        qkv = jnp.dot(rows, qkv_weight, preferred_element_type=jnp.float32).astype(jnp.bfloat16)
        queries = qkv[:, :D].reshape(SEQ, HEADS, HEAD_DIM).astype(jnp.float32)
        keys_part = qkv[:, D:2 * D].reshape(SEQ, HEADS, HEAD_DIM).astype(jnp.float32)
        values_part = qkv[:, 2 * D:].reshape(SEQ, HEADS, HEAD_DIM).astype(jnp.float32)
        scores = jnp.einsum('qhd,khd->hqk', queries, keys_part) * scale
        probs = jax.nn.softmax(scores, axis=-1).astype(jnp.bfloat16)
        context = jnp.einsum('hqk,khd->qhd', probs.astype(jnp.float32), values_part).astype(jnp.bfloat16)
        return jnp.dot(context.reshape(SEQ, D), mix_weight, preferred_element_type=jnp.float32).astype(jnp.bfloat16)
    attn_branch = lax.map(attend, attn_normed.reshape(total // SEQ, SEQ, D)).reshape(total, D)
    return (moe_out, attn_branch)
```

```python
import functools

import jax
import jax.numpy as jnp
from jax import lax
from jax.experimental import pallas as pl
from jax.experimental.pallas import tpu as pltpu
from jax.sharding import PartitionSpec as P

HEAD_DIM = 64
SEQ = 512
LANES = 128
DIGIT = 32
EPSILON = 1e-06
BF16 = jnp.bfloat16
F32 = jnp.float32
I32 = jnp.int32
NT = (((1,), (1,)), ((), ()))
MIB = 1 << 20


def iota(shape, axis):
    return lax.broadcasted_iota(I32, shape, axis)


def dot(a, b):
    return jnp.dot(a, b, preferred_element_type=F32)


def dot_nt(a, b):
    return lax.dot_general(a, b, NT, preferred_element_type=F32)


def one(mask):
    return jnp.where(mask, 1.0, 0.0).astype(BF16)


def rms_scale(values, gain):
    widened = values.astype(F32)
    power = jnp.mean(widened * widened, axis=-1, keepdims=True)
    return (widened * lax.rsqrt(power + EPSILON) * gain).astype(BF16)


def earlier(rows):
    return one(iota((rows, rows), 0) < iota((rows, rows), 1))


def permute(place, rows, source, low=0, count=None):
    count = rows if count is None else count
    return dot(one(iota((count, rows), 0) + low == place), source)


def to_blocks(onehot, rank, fields, per):
    rows = rank.shape[1]
    lane = iota((LANES, rows), 0)
    value = jnp.zeros((LANES, rows), F32)
    for k, field in enumerate(fields):
        value = jnp.where(lane == rank + k * per, field, value)
    return dot_nt(onehot, value.astype(BF16))


def spread(blocks, rows, per):
    devices = blocks.shape[0]
    owner = one(iota((rows, devices), 0) // per == iota((rows, devices), 1))
    lanes = dot(owner, blocks.astype(BF16))
    keep = iota((rows, LANES), 1) % per == iota((rows, LANES), 0) % per
    return jnp.where(keep, lanes, 0.0).astype(BF16)


def field_rows(spreaded, per):
    pick = one(iota((8, LANES), 1) // per == iota((8, LANES), 0))
    return dot_nt(pick, spreaded)


def dispatch_kernel(devices, id_ref, dest_ref, gate_ref, tok_ref, out_ref, meta_ref):
    rows = tok_ref.shape[0]
    per = rows // devices
    ids = id_ref[...]
    dest = dest_ref[...]
    target = ids // 2
    local = ids - target * 2
    owner = dest // rows
    place = dest - owner * rows
    onehot = one(iota((devices, rows), 0) == target)
    counts = dot(onehot, earlier(rows))
    rank = jnp.sum(onehot.astype(F32) * counts, axis=0, keepdims=True).astype(I32)
    fields = [
        (local * DIGIT + place % DIGIT).astype(F32),
        (place // DIGIT).astype(F32),
        owner.astype(F32),
        gate_ref[...].astype(F32),
    ]
    meta_ref[...] = to_blocks(onehot, rank, fields, per)
    position = target * per + rank
    step = rows // 4
    for i in range(4):
        part = permute(position, rows, tok_ref[...], i * step, step)
        out_ref[i * step : (i + 1) * step, :] = part.astype(BF16)


def expert_kernel(
    devices, x_ref, meta_ref, gain_ref, in_ref, out_ref, y_ref, meta2_ref, xs, inputs, total, info, places
):
    rows, width = x_ref.shape
    per = rows // devices
    cap = inputs.shape[1]
    expert, chunk = pl.program_id(0), pl.program_id(1)

    @pl.when((expert == 0) & (chunk == 0))
    def _():
        spreaded = spread(meta_ref[...], rows, per)
        fields = field_rows(spreaded, per)
        code = fields[0:1].astype(I32)
        high = fields[1:2].astype(I32)
        owner = fields[2:3].astype(I32)
        local = code // DIGIT
        low = code - local * DIGIT
        onehot = one(iota((devices, rows), 0) == owner)
        first = one(jnp.broadcast_to(local == 0, (8, rows)))
        upper = earlier(rows)
        counts = dot(onehot, upper)
        rank2 = jnp.sum(onehot.astype(F32) * counts, axis=0, keepdims=True).astype(I32)
        meta2_ref[...] = to_blocks(onehot, rank2, [low.astype(F32), high.astype(F32)], per)
        leave = owner * per + rank2
        before = dot(first, upper)[0:1].astype(I32)
        number = jnp.sum(jnp.where(local == 0, 1.0, 0.0), axis=1, keepdims=True).astype(I32)
        position = jnp.where(local == 0, before, number + iota((1, rows), 1) - before)
        sort = one(iota((rows, rows), 0) == position)
        digit = iota((8, rows), 0)
        leave_digits = jnp.where(digit == 0, leave // DIGIT, leave % DIGIT).astype(F32)
        places[...] = dot_nt(leave_digits.astype(BF16), sort)
        put = one(iota((LANES, LANES), 0) // per == iota((LANES, LANES), 1))
        columns = dot(spreaded, put).astype(BF16)
        info[...] = dot(sort, columns)
        step = rows // 4
        for i in range(4):
            part = slice(i * step, (i + 1) * step)
            sorted_rows = dot(sort[part], x_ref[...]).astype(BF16)
            xs[part] = sorted_rows
            normed = rms_scale(sorted_rows, gain_ref[...])
            is_first = iota((step, 1), 0) + i * step < number
            none = jnp.zeros_like(normed)
            if (i + 1) * step <= cap:
                inputs[0, i * step : (i + 1) * step] = jnp.where(is_first, normed, none)
            if i * step >= rows - cap:
                low_row = i * step - (rows - cap)
                inputs[1, low_row : low_row + step] = jnp.where(is_first, none, normed)
        total[...] = jnp.zeros_like(total)

    base = pl.multiple_of(expert * (rows - cap), rows - cap)
    hidden = jnp.maximum(dot(inputs[expert], in_ref[0]), 0.0).astype(BF16)
    total[pl.ds(base, cap), :] += dot(hidden, out_ref[0])

    @pl.when((expert == 1) & (chunk == pl.num_programs(1) - 1))
    def _():
        gate = info[:, 3:4]
        result = total[...].astype(BF16).astype(F32)
        xs[...] = (xs[...].astype(F32) + gate * result).astype(BF16)
        leave = (places[0:1] * DIGIT + places[1:2]).astype(I32)
        step = rows // 4
        for i in range(4):
            part = permute(leave, rows, xs[...], i * step, step)
            y_ref[i * step : (i + 1) * step, :] = part.astype(BF16)


def attention_kernel(devices, x_ref, meta_ref, gain_ref, qkv_ref, mix_ref, moe_ref, branch_ref, qkv, context):
    rows, width = x_ref.shape
    per = rows // devices
    seq = moe_ref.shape[0]
    fields = field_rows(spread(meta_ref[...], rows, per), per)
    place = (fields[1:2] * DIGIT + fields[0:1]).astype(I32)
    moved = permute(place, rows, x_ref[...], pl.program_id(0) * seq, seq).astype(BF16)
    moe_ref[...] = moved
    normed = rms_scale(moved, gain_ref[...])
    for i in range(3):
        part = slice(i * width, (i + 1) * width)
        qkv[:, part] = dot(normed, qkv_ref[:, part]).astype(BF16)
    scale = 1.0 / HEAD_DIM**0.5
    left = iota((seq, LANES), 1) < HEAD_DIM
    ones = jnp.ones((seq, LANES), BF16)
    for pair in range(width // LANES):
        at = pair * LANES
        queries = qkv[:, at : at + LANES] * jnp.asarray(scale, BF16)
        keys = qkv[:, width + at : width + at + LANES]
        values = jnp.concatenate([qkv[:, 2 * width + at : 2 * width + at + LANES], ones], axis=1)
        halves = []
        for mask in (left, jnp.logical_not(left)):
            scores = dot_nt(jnp.where(mask, queries, jnp.zeros_like(queries)), keys)
            peak = jnp.max(scores, axis=1, keepdims=True)
            weights = jnp.exp(scores - peak).astype(BF16)
            mixed = dot(weights, values)
            halves.append(mixed[:, :LANES] / mixed[:, LANES:])
        context[:, at : at + LANES] = jnp.where(left, halves[0], halves[1]).astype(BF16)
    branch_ref[...] = dot(context[...], mix_ref[...]).astype(BF16)


def exchange_kernel(sizes, x_ref, m_ref, y_ref, n_ref, send, recv, send_meta, recv_meta, own):
    n_row, n_col = sizes
    devices = n_row * n_col
    per = x_ref.shape[0] // devices
    me = lax.axis_index("row") * n_col + lax.axis_index("col")

    def peer_of(i):
        return lax.rem(me + i, devices)

    def coords(device):
        return (device // n_col, lax.rem(device, n_col))

    def block(ref, device):
        return ref.at[pl.ds(pl.multiple_of(device * per, per), per)]

    barrier = pltpu.get_barrier_semaphore()

    def greet(i, carry):
        pl.semaphore_signal(
            barrier, inc=1, device_id=coords(peer_of(i)), device_id_type=pl.DeviceIdType.MESH
        )
        return carry

    lax.fori_loop(1, devices, greet, 0)
    mine = [
        pltpu.make_async_copy(block(x_ref, me), block(y_ref, me), own.at[0]),
        pltpu.make_async_copy(m_ref.at[me], n_ref.at[me], own.at[1]),
    ]
    for copy in mine:
        copy.start()
    pl.semaphore_wait(barrier, devices - 1)

    def copies(i, target, landing):
        peer = peer_of(i)
        return (
            pltpu.make_async_remote_copy(
                src_ref=m_ref.at[peer],
                dst_ref=n_ref.at[landing],
                send_sem=send_meta.at[i],
                recv_sem=recv_meta.at[i],
                device_id=coords(target),
                device_id_type=pl.DeviceIdType.MESH,
            ),
            pltpu.make_async_remote_copy(
                src_ref=block(x_ref, peer),
                dst_ref=block(y_ref, landing),
                send_sem=send.at[i],
                recv_sem=recv.at[i],
                device_id=coords(target),
                device_id_type=pl.DeviceIdType.MESH,
            ),
        )

    def begin(i, carry):
        for copy in copies(i, peer_of(i), me):
            copy.start()
        return carry

    lax.fori_loop(1, devices, begin, 0)

    def finish(i, carry):
        source = lax.rem(me + devices - i, devices)
        for copy in copies(i, peer_of(i), source):
            copy.wait_send()
            copy.wait_recv()
        return carry

    lax.fori_loop(1, devices, finish, 0)
    for copy in mine:
        copy.wait()


def exchange(x, meta, sizes, collective_id):
    devices = sizes[0] * sizes[1]
    rows, width = x.shape
    per = rows // devices
    meta = meta.reshape(devices, 1, LANES)
    if per % 16:
        y = lax.all_to_all(
            x.reshape(devices, per, width), ("row", "col"), split_axis=0, concat_axis=0, tiled=True
        )
        n = lax.all_to_all(meta, ("row", "col"), split_axis=0, concat_axis=0, tiled=True)
        return y.reshape(rows, width), n.reshape(devices, LANES)
    anywhere = pl.BlockSpec(memory_space=pl.ANY)
    y, n = pl.pallas_call(
        functools.partial(exchange_kernel, sizes),
        out_shape=(
            jax.ShapeDtypeStruct(x.shape, x.dtype),
            jax.ShapeDtypeStruct(meta.shape, meta.dtype),
        ),
        in_specs=[anywhere] * 2,
        out_specs=(anywhere, anywhere),
        scratch_shapes=[pltpu.SemaphoreType.DMA((devices,))] * 4 + [pltpu.SemaphoreType.DMA((2,))],
        compiler_params=pltpu.CompilerParams(collective_id=collective_id, has_side_effects=True),
        name="exchange%d" % collective_id,
    )(x, meta)
    return y, n.reshape(devices, LANES)


def whole(shape):
    return pl.BlockSpec(shape, lambda *_: (0,) * len(shape))


def shards(
    sizes,
    tokens,
    gate_prob,
    expert_id,
    dest_row,
    ff_gain,
    expert_in,
    expert_out,
    attn_gain,
    qkv_weight,
    mix_weight,
):
    rows, width = tokens.shape
    devices = sizes[0] * sizes[1]
    hidden = expert_in.shape[2]
    cap = rows * 3 // 4
    qkv_full = lax.all_gather(qkv_weight, "row", axis=1, tiled=True)
    mix_full = lax.all_gather(mix_weight, "row", axis=1, tiled=True)
    meta_shape = jax.ShapeDtypeStruct((devices, LANES), F32)
    rows_shape = jax.ShapeDtypeStruct((rows, width), BF16)

    leaving, meta = pl.pallas_call(
        functools.partial(dispatch_kernel, devices),
        out_shape=(rows_shape, meta_shape),
        compiler_params=pltpu.CompilerParams(vmem_limit_bytes=32 * MIB),
        name="dispatch",
    )(
        expert_id.reshape(1, rows),
        dest_row.reshape(1, rows),
        gate_prob.reshape(1, rows),
        tokens,
    )
    arrived, meta = exchange(leaving, meta, sizes, 1)

    chunk = hidden // 4
    leaving, meta = pl.pallas_call(
        functools.partial(expert_kernel, devices),
        out_shape=(rows_shape, meta_shape),
        grid=(2, hidden // chunk),
        in_specs=[
            whole((rows, width)),
            whole((devices, LANES)),
            whole((1, width)),
            pl.BlockSpec((1, width, chunk), lambda e, c: (e, 0, c)),
            pl.BlockSpec((1, chunk, width), lambda e, c: (e, c, 0)),
        ],
        out_specs=(whole((rows, width)), whole((devices, LANES))),
        scratch_shapes=[
            pltpu.VMEM((rows, width), BF16),
            pltpu.VMEM((2, cap, width), BF16),
            pltpu.VMEM((rows, width), F32),
            pltpu.VMEM((rows, LANES), F32),
            pltpu.VMEM((8, rows), F32),
        ],
        compiler_params=pltpu.CompilerParams(vmem_limit_bytes=48 * MIB),
        name="experts",
    )(arrived, meta, ff_gain.reshape(1, width), expert_in, expert_out)
    arrived, meta = exchange(leaving, meta, sizes, 2)

    return pl.pallas_call(
        functools.partial(attention_kernel, devices),
        out_shape=(rows_shape, rows_shape),
        grid=(rows // SEQ,),
        in_specs=[
            whole((rows, width)),
            whole((devices, LANES)),
            whole((1, width)),
            whole((width, 3 * width)),
            whole((width, width)),
        ],
        out_specs=(
            pl.BlockSpec((SEQ, width), lambda s: (s, 0)),
            pl.BlockSpec((SEQ, width), lambda s: (s, 0)),
        ),
        scratch_shapes=[
            pltpu.VMEM((SEQ, 3 * width), BF16),
            pltpu.VMEM((SEQ, width), BF16),
        ],
        compiler_params=pltpu.CompilerParams(vmem_limit_bytes=48 * MIB),
        name="attention",
    )(arrived, meta, attn_gain.reshape(1, width), qkv_full, mix_full)


def solution(mesh):
    placed = (
        P(("row", "col"), None),
        P(("row", "col")),
        P(("row", "col")),
        P(("row", "col")),
        P(),
        P(("row", "col"), None, None),
        P(("row", "col"), None, None),
        P(),
        P(None, "row"),
        P(None, "row"),
    )
    sizes = (mesh.shape["row"], mesh.shape["col"])
    return jax.shard_map(
        functools.partial(shards, sizes),
        mesh=mesh,
        in_specs=placed,
        out_specs=(P(("row", "col"), None), P(("row", "col"), None)),
        check_vma=False,
    )
```

```python
import functools

import jax
import jax.numpy as jnp
from jax import lax
from jax.experimental import pallas as pl
from jax.experimental.pallas import tpu as pltpu
from jax.sharding import PartitionSpec as P

HEAD_DIM = 64
SEQ = 512
LANES = 128
DIGIT = 32
EPSILON = 1e-06
BF16 = jnp.bfloat16
F32 = jnp.float32
I32 = jnp.int32
NT = (((1,), (1,)), ((), ()))
MIB = 1 << 20


def iota(shape, axis):
    return lax.broadcasted_iota(I32, shape, axis)


def dot(a, b):
    return jnp.dot(a, b, preferred_element_type=F32)


def dot_nt(a, b):
    return lax.dot_general(a, b, NT, preferred_element_type=F32)


def one(mask):
    return jnp.where(mask, 1.0, 0.0).astype(BF16)


def rms_scale(values, gain):
    widened = values.astype(F32)
    power = jnp.mean(widened * widened, axis=-1, keepdims=True)
    return (widened * lax.rsqrt(power + EPSILON) * gain).astype(BF16)


def earlier(rows):
    return one(iota((rows, rows), 0) < iota((rows, rows), 1))


def permute(place, rows, source, low=0, count=None):
    count = rows if count is None else count
    return dot(one(iota((count, rows), 0) + low == place), source)


def to_blocks(onehot, rank, fields, per):
    rows = rank.shape[1]
    lane = iota((LANES, rows), 0)
    value = jnp.zeros((LANES, rows), F32)
    for k, field in enumerate(fields):
        value = jnp.where(lane == rank + k * per, field, value)
    return dot_nt(onehot, value.astype(BF16))


def spread(blocks, rows, per):
    devices = blocks.shape[0]
    owner = one(iota((rows, devices), 0) // per == iota((rows, devices), 1))
    lanes = dot(owner, blocks.astype(BF16))
    keep = iota((rows, LANES), 1) % per == iota((rows, LANES), 0) % per
    return jnp.where(keep, lanes, 0.0).astype(BF16)


def field_rows(spreaded, per):
    pick = one(iota((8, LANES), 1) // per == iota((8, LANES), 0))
    return dot_nt(pick, spreaded)


def dispatch_kernel(devices, id_ref, dest_ref, gate_ref, tok_ref, out_ref, meta_ref):
    rows = tok_ref.shape[0]
    per = rows // devices
    ids = id_ref[...]
    dest = dest_ref[...]
    target = ids // 2
    local = ids - target * 2
    owner = dest // rows
    place = dest - owner * rows
    onehot = one(iota((devices, rows), 0) == target)
    counts = dot(onehot, earlier(rows))
    rank = jnp.sum(onehot.astype(F32) * counts, axis=0, keepdims=True).astype(I32)
    fields = [
        (local * DIGIT + place % DIGIT).astype(F32),
        (place // DIGIT).astype(F32),
        owner.astype(F32),
        gate_ref[...].astype(F32),
    ]
    meta_ref[...] = to_blocks(onehot, rank, fields, per)
    position = target * per + rank
    step = rows // 4
    for i in range(4):
        part = permute(position, rows, tok_ref[...], i * step, step)
        out_ref[i * step : (i + 1) * step, :] = part.astype(BF16)


def expert_kernel(
    devices, x_ref, meta_ref, gain_ref, in_ref, out_ref, y_ref, meta2_ref, xs, inputs, total, info, places, split
):
    rows, width = x_ref.shape
    per = rows // devices
    cap = inputs.shape[1]
    expert, chunk = pl.program_id(0), pl.program_id(1)

    @pl.when((expert == 0) & (chunk == 0))
    def _():
        spreaded = spread(meta_ref[...], rows, per)
        fields = field_rows(spreaded, per)
        code = fields[0:1].astype(I32)
        high = fields[1:2].astype(I32)
        owner = fields[2:3].astype(I32)
        local = code // DIGIT
        low = code - local * DIGIT
        onehot = one(iota((devices, rows), 0) == owner)
        first = one(jnp.broadcast_to(local == 0, (8, rows)))
        upper = earlier(rows)
        counts = dot(onehot, upper)
        rank2 = jnp.sum(onehot.astype(F32) * counts, axis=0, keepdims=True).astype(I32)
        meta2_ref[...] = to_blocks(onehot, rank2, [low.astype(F32), high.astype(F32)], per)
        leave = owner * per + rank2
        before = dot(first, upper)[0:1].astype(I32)
        number = jnp.sum(jnp.where(local == 0, 1.0, 0.0), axis=1, keepdims=True).astype(I32)
        position = jnp.where(local == 0, before, number + iota((1, rows), 1) - before)
        sort = one(iota((rows, rows), 0) == position)
        digit = iota((8, rows), 0)
        leave_digits = jnp.where(digit == 0, leave // DIGIT, leave % DIGIT).astype(F32)
        places[...] = dot_nt(leave_digits.astype(BF16), sort)
        put = one(iota((LANES, LANES), 0) // per == iota((LANES, LANES), 1))
        columns = dot(spreaded, put).astype(BF16)
        info[...] = dot(sort, columns)
        step = rows // 4
        for i in range(4):
            part = slice(i * step, (i + 1) * step)
            sorted_rows = dot(sort[part], x_ref[...]).astype(BF16)
            xs[part] = sorted_rows
            normed = rms_scale(sorted_rows, gain_ref[...])
            is_first = iota((step, 1), 0) + i * step < number
            none = jnp.zeros_like(normed)
            if (i + 1) * step <= cap:
                inputs[0, i * step : (i + 1) * step] = jnp.where(is_first, normed, none)
            if i * step >= rows - cap:
                low_row = i * step - (rows - cap)
                inputs[1, low_row : low_row + step] = jnp.where(is_first, none, normed)
        total[...] = jnp.zeros_like(total)
        split[0] = jnp.sum(jnp.where(local == 0, 1.0, 0.0)).astype(I32)

    tile = rows // 4
    own_rows = jnp.where(expert == 0, split[0], rows - split[0])
    for tiles in range(1, cap // tile + 1):
        size = tiles * tile

        @pl.when((own_rows <= size) & (own_rows > size - tile))
        def _():
            source = pl.multiple_of(expert * (cap - size), tile)
            base = pl.multiple_of(expert * (rows - size), tile)
            wide = dot(inputs[expert, pl.ds(source, size)], in_ref[0])
            hidden = jnp.maximum(wide, 0.0).astype(BF16)
            total[pl.ds(base, size), :] += dot(hidden, out_ref[0])

    @pl.when((expert == 1) & (chunk == pl.num_programs(1) - 1))
    def _():
        gate = info[:, 3:4]
        result = total[...].astype(BF16).astype(F32)
        xs[...] = (xs[...].astype(F32) + gate * result).astype(BF16)
        leave = (places[0:1] * DIGIT + places[1:2]).astype(I32)
        step = rows // 4
        for i in range(4):
            part = permute(leave, rows, xs[...], i * step, step)
            y_ref[i * step : (i + 1) * step, :] = part.astype(BF16)


def attention_kernel(devices, x_ref, meta_ref, gain_ref, qkv_ref, mix_ref, moe_ref, branch_ref, qkv, context):
    rows, width = x_ref.shape
    per = rows // devices
    seq = moe_ref.shape[0]
    fields = field_rows(spread(meta_ref[...], rows, per), per)
    place = (fields[1:2] * DIGIT + fields[0:1]).astype(I32)
    moved = permute(place, rows, x_ref[...], pl.program_id(0) * seq, seq).astype(BF16)
    moe_ref[...] = moved
    normed = rms_scale(moved, gain_ref[...])
    for i in range(3):
        part = slice(i * width, (i + 1) * width)
        qkv[:, part] = dot_nt(normed, qkv_ref[part]).astype(BF16)
    scale = 1.0 / HEAD_DIM**0.5
    left = iota((seq, LANES), 1) < HEAD_DIM
    ones = jnp.ones((seq, LANES), BF16)
    for pair in range(width // LANES):
        at = pair * LANES
        queries = qkv[:, at : at + LANES] * jnp.asarray(scale, BF16)
        keys = qkv[:, width + at : width + at + LANES]
        values = jnp.concatenate([qkv[:, 2 * width + at : 2 * width + at + LANES], ones], axis=1)
        halves = []
        for mask in (left, jnp.logical_not(left)):
            scores = dot_nt(jnp.where(mask, queries, jnp.zeros_like(queries)), keys)
            peak = jnp.max(scores, axis=1, keepdims=True)
            weights = jnp.exp(scores - peak).astype(BF16)
            mixed = dot(weights, values)
            halves.append(mixed[:, :LANES] / mixed[:, LANES:])
        context[:, at : at + LANES] = jnp.where(left, halves[0], halves[1]).astype(BF16)
    branch_ref[...] = dot_nt(context[...], mix_ref[...]).astype(BF16)


def peers(sizes):
    n_row, n_col = sizes
    devices = n_row * n_col
    row, col = lax.axis_index("row"), lax.axis_index("col")
    me = row * n_col + col

    def peer_of(i):
        return lax.rem(me + i, devices)

    def coords(device):
        return (device // n_col, lax.rem(device, n_col))

    return row, col, me, peer_of, coords


def greet_all(sizes):
    _, _, _, peer_of, coords = peers(sizes)
    barrier = pltpu.get_barrier_semaphore()

    def greet(i, carry):
        pl.semaphore_signal(
            barrier, inc=1, device_id=coords(peer_of(i)), device_id_type=pl.DeviceIdType.MESH
        )
        return carry

    lax.fori_loop(1, sizes[0] * sizes[1], greet, 0)
    return barrier


def remote(source, landing, send, recv, device):
    return pltpu.make_async_remote_copy(
        src_ref=source,
        dst_ref=landing,
        send_sem=send,
        recv_sem=recv,
        device_id=device,
        device_id_type=pl.DeviceIdType.MESH,
    )


def rows_exchange(sizes, x_ref, m_ref, y_ref, n_ref, send, recv, send_meta, recv_meta, own):
    devices = sizes[0] * sizes[1]
    per = x_ref.shape[0] // devices
    _, _, me, peer_of, coords = peers(sizes)

    def block(ref, device):
        return ref.at[pl.ds(pl.multiple_of(device * per, per), per)]

    def mine():
        return (
            pltpu.make_async_copy(block(x_ref, me), block(y_ref, me), own.at[0]),
            pltpu.make_async_copy(m_ref.at[me], n_ref.at[me], own.at[1]),
        )

    def copies(i, landing):
        peer = peer_of(i)
        target = coords(peer)
        return (
            remote(m_ref.at[peer], n_ref.at[landing], send_meta.at[i], recv_meta.at[i], target),
            remote(block(x_ref, peer), block(y_ref, landing), send.at[i], recv.at[i], target),
        )

    def start():
        def begin(i, carry):
            for copy in copies(i, me):
                copy.start()
            return carry

        for copy in mine():
            copy.start()
        lax.fori_loop(1, devices, begin, 0)

    def end():
        def finish(i, carry):
            for copy in copies(i, lax.rem(me + devices - i, devices)):
                copy.wait_send()
                copy.wait_recv()
            return carry

        for copy in mine():
            copy.wait()
        lax.fori_loop(1, devices, finish, 0)

    return start, end


def exchange1_kernel(sizes, x_ref, m_ref, w_ref, y_ref, n_ref, held_ref, *sems):
    chips = sizes[0] // 2
    row, col, _, _, _ = peers(sizes)
    chip, core = row // 2, lax.rem(row, 2)
    send_w, recv_w = sems[5:]
    start, end = rows_exchange(sizes, x_ref, m_ref, y_ref, n_ref, *sems[:5])
    barrier = greet_all(sizes)
    own = pltpu.make_async_copy(w_ref, held_ref.at[chip], send_w.at[0])
    own.start()
    pl.semaphore_wait(barrier, sizes[0] * sizes[1] - 1)
    start()

    def weights(i, landing):
        target = (lax.rem(chip + i, chips) * 2 + core, col)
        return remote(w_ref, held_ref.at[landing], send_w.at[i], recv_w.at[i], target)

    for i in range(1, chips):
        weights(i, chip).start()
    own.wait()
    for i in range(1, chips):
        weights(i, lax.rem(chip + chips - i, chips)).wait()
    end()


def exchange2_kernel(
    sizes, x_ref, m_ref, held_ref, mix_ref, y_ref, n_ref, wide_ref, full_ref, *sems
):
    n_row = sizes[0]
    chips, columns, _ = held_ref.shape
    mix_columns = mix_ref.shape[0]
    row, col, _, _, _ = peers(sizes)
    core = lax.rem(row, 2)
    local_w, send_w, recv_w, send_x, recv_x = sems[5:]
    start, end = rows_exchange(sizes, x_ref, m_ref, y_ref, n_ref, *sems[:5])
    barrier = greet_all(sizes)

    def part(ref, index, size):
        return ref.at[pl.ds(pl.multiple_of(index * size, size), size)]

    owned = [
        pltpu.make_async_copy(held_ref.at[c], part(wide_ref, 2 * c + core, columns), local_w.at[c])
        for c in range(chips)
    ]
    owned.append(pltpu.make_async_copy(mix_ref, part(full_ref, row, mix_columns), local_w.at[chips]))
    for copy in owned:
        copy.start()
    pl.semaphore_wait(barrier, sizes[0] * sizes[1] - 1)
    sibling = (row + 1 - 2 * core, col)

    def weights(c, side):
        landing = part(wide_ref, 2 * c + side, columns)
        return remote(held_ref.at[c], landing, send_w.at[c], recv_w.at[c], sibling)

    def mixing(i, landing):
        target = (lax.rem(row + i, n_row), col)
        landing = part(full_ref, landing, mix_columns)
        return remote(mix_ref, landing, send_x.at[i], recv_x.at[i], target)

    start()
    for c in range(chips):
        weights(c, core).start()
    for i in range(1, n_row):
        mixing(i, row).start()
    for copy in owned:
        copy.wait()
    for c in range(chips):
        weights(c, 1 - core).wait()
    for i in range(1, n_row):
        mixing(i, lax.rem(row + n_row - i, n_row)).wait()
    end()


def exchange_first(sizes, x, meta, qkv_weight, mix_weight):
    devices = sizes[0] * sizes[1]
    rows, width = x.shape
    meta = meta.reshape(devices, 1, LANES)
    if rows // devices % 16 or sizes[0] % 2:
        held = (
            lax.all_gather(qkv_weight, "row", axis=0, tiled=True),
            lax.all_gather(mix_weight, "row", axis=0, tiled=True),
        )
        return *all_to_all(devices, x, meta), held
    vmem = pl.BlockSpec()
    hbm = pl.BlockSpec(memory_space=pl.ANY)
    chips = sizes[0] // 2
    y, n, held = pl.pallas_call(
        functools.partial(exchange1_kernel, sizes),
        out_shape=(
            jax.ShapeDtypeStruct(x.shape, x.dtype),
            jax.ShapeDtypeStruct(meta.shape, meta.dtype),
            jax.ShapeDtypeStruct((chips, *qkv_weight.shape), BF16),
        ),
        in_specs=[vmem, vmem, hbm],
        out_specs=(vmem, vmem, hbm),
        scratch_shapes=[pltpu.SemaphoreType.DMA((devices,))] * 4
        + [pltpu.SemaphoreType.DMA((2,))]
        + [pltpu.SemaphoreType.DMA((chips,))] * 2,
        compiler_params=pltpu.CompilerParams(
            collective_id=1, has_side_effects=True, vmem_limit_bytes=32 * MIB
        ),
        name="exchange1",
    )(x, meta, qkv_weight)
    return y, n.reshape(devices, LANES), held


def all_to_all(devices, x, meta):
    rows, width = x.shape
    y, n = (
        lax.all_to_all(part, ("row", "col"), split_axis=0, concat_axis=0, tiled=True)
        for part in (x.reshape(devices, rows // devices, width), meta)
    )
    return y.reshape(rows, width), n.reshape(devices, LANES)


def exchange_second(sizes, x, meta, held, mix_weight):
    devices = sizes[0] * sizes[1]
    rows, width = x.shape
    meta = meta.reshape(devices, 1, LANES)
    if rows // devices % 16 or sizes[0] % 2:
        return *all_to_all(devices, x, meta), *held
    vmem = pl.BlockSpec()
    hbm = pl.BlockSpec(memory_space=pl.ANY)
    n_row = sizes[0]
    chips, columns, depth = held.shape
    y, n, wide, full = pl.pallas_call(
        functools.partial(exchange2_kernel, sizes),
        out_shape=(
            jax.ShapeDtypeStruct(x.shape, x.dtype),
            jax.ShapeDtypeStruct(meta.shape, meta.dtype),
            jax.ShapeDtypeStruct((n_row * columns, depth), BF16),
            jax.ShapeDtypeStruct((n_row * mix_weight.shape[0], depth), BF16),
        ),
        in_specs=[vmem, vmem, hbm, hbm],
        out_specs=(vmem,) * 4,
        scratch_shapes=[pltpu.SemaphoreType.DMA((devices,))] * 4
        + [pltpu.SemaphoreType.DMA((2,))]
        + [pltpu.SemaphoreType.DMA((chips + 1,))]
        + [pltpu.SemaphoreType.DMA((chips,))] * 2
        + [pltpu.SemaphoreType.DMA((n_row,))] * 2,
        compiler_params=pltpu.CompilerParams(
            collective_id=2, has_side_effects=True, vmem_limit_bytes=40 * MIB
        ),
        name="exchange2",
    )(x, meta, held, mix_weight)
    return y, n.reshape(devices, LANES), wide, full


def whole(shape):
    return pl.BlockSpec(shape, lambda *_: (0,) * len(shape))


def shards(
    sizes,
    tokens,
    gate_prob,
    expert_id,
    dest_row,
    ff_gain,
    expert_in,
    expert_out,
    attn_gain,
    qkv_weight,
    mix_weight,
):
    rows, width = tokens.shape
    devices = sizes[0] * sizes[1]
    hidden = expert_in.shape[2]
    cap = rows * 3 // 4
    meta_shape = jax.ShapeDtypeStruct((devices, LANES), F32)
    qkv_weight, mix_weight = qkv_weight.T, mix_weight.T
    rows_shape = jax.ShapeDtypeStruct((rows, width), BF16)

    leaving, meta = pl.pallas_call(
        functools.partial(dispatch_kernel, devices),
        out_shape=(rows_shape, meta_shape),
        compiler_params=pltpu.CompilerParams(vmem_limit_bytes=32 * MIB),
        name="dispatch",
    )(
        expert_id.reshape(1, rows),
        dest_row.reshape(1, rows),
        gate_prob.reshape(1, rows),
        tokens,
    )
    arrived, meta, held = exchange_first(sizes, leaving, meta, qkv_weight, mix_weight)

    chunk = hidden // 4
    leaving, meta = pl.pallas_call(
        functools.partial(expert_kernel, devices),
        out_shape=(rows_shape, meta_shape),
        grid=(2, hidden // chunk),
        in_specs=[
            whole((rows, width)),
            whole((devices, LANES)),
            whole((1, width)),
            pl.BlockSpec((1, width, chunk), lambda e, c: (e, 0, c)),
            pl.BlockSpec((1, chunk, width), lambda e, c: (e, c, 0)),
        ],
        out_specs=(whole((rows, width)), whole((devices, LANES))),
        scratch_shapes=[
            pltpu.VMEM((rows, width), BF16),
            pltpu.VMEM((2, cap, width), BF16),
            pltpu.VMEM((rows, width), F32),
            pltpu.VMEM((rows, LANES), F32),
            pltpu.VMEM((8, rows), F32),
            pltpu.SMEM((1,), I32),
        ],
        compiler_params=pltpu.CompilerParams(vmem_limit_bytes=48 * MIB),
        name="experts",
    )(arrived, meta, ff_gain.reshape(1, width), expert_in, expert_out)
    arrived, meta, qkv_full, mix_full = exchange_second(sizes, leaving, meta, held, mix_weight)

    return pl.pallas_call(
        functools.partial(attention_kernel, devices),
        out_shape=(rows_shape, rows_shape),
        grid=(rows // SEQ,),
        in_specs=[
            whole((rows, width)),
            whole((devices, LANES)),
            whole((1, width)),
            whole((3 * width, width)),
            whole((width, width)),
        ],
        out_specs=(
            pl.BlockSpec((SEQ, width), lambda s: (s, 0)),
            pl.BlockSpec((SEQ, width), lambda s: (s, 0)),
        ),
        scratch_shapes=[
            pltpu.VMEM((SEQ, 3 * width), BF16),
            pltpu.VMEM((SEQ, width), BF16),
        ],
        compiler_params=pltpu.CompilerParams(vmem_limit_bytes=32 * MIB),
        name="attention",
    )(arrived, meta, attn_gain.reshape(1, width), qkv_full, mix_full)


def solution(mesh):
    placed = (
        P(("row", "col"), None),
        P(("row", "col")),
        P(("row", "col")),
        P(("row", "col")),
        P(),
        P(("row", "col"), None, None),
        P(("row", "col"), None, None),
        P(),
        P(None, "row"),
        P(None, "row"),
    )
    sizes = (mesh.shape["row"], mesh.shape["col"])
    return jax.shard_map(
        functools.partial(shards, sizes),
        mesh=mesh,
        in_specs=placed,
        out_specs=(P(("row", "col"), None), P(("row", "col"), None)),
        check_vma=False,
    )
```

```python
import functools

import jax
import jax.numpy as jnp
from jax import lax
from jax.experimental import pallas as pl
from jax.experimental.pallas import tpu as pltpu
from jax.sharding import PartitionSpec as P

HEAD_DIM = 64
SEQ = 512
LANES = 128
DIGIT = 32
EPSILON = 1e-06
BF16 = jnp.bfloat16
F32 = jnp.float32
I32 = jnp.int32
NT = (((1,), (1,)), ((), ()))
MIB = 1 << 20


def iota(shape, axis):
    return lax.broadcasted_iota(I32, shape, axis)


def dot(a, b):
    return jnp.dot(a, b, preferred_element_type=F32)


def dot_nt(a, b):
    return lax.dot_general(a, b, NT, preferred_element_type=F32)


def one(mask):
    return jnp.where(mask, 1.0, 0.0).astype(BF16)


def rms_scale(values, gain):
    widened = values.astype(F32)
    power = jnp.mean(widened * widened, axis=-1, keepdims=True)
    return (widened * lax.rsqrt(power + EPSILON) * gain).astype(BF16)


def earlier(rows):
    return one(iota((rows, rows), 0) < iota((rows, rows), 1))


def permute(place, rows, source, low=0, count=None):
    count = rows if count is None else count
    return dot(one(iota((count, rows), 0) + low == place), source)


def to_blocks(onehot, rank, fields, per):
    rows = rank.shape[1]
    lane = iota((LANES, rows), 0)
    value = jnp.zeros((LANES, rows), F32)
    for k, field in enumerate(fields):
        value = jnp.where(lane == rank + k * per, field, value)
    return dot_nt(onehot, value.astype(BF16))


def spread(blocks, rows, per):
    devices = blocks.shape[0]
    owner = one(iota((rows, devices), 0) // per == iota((rows, devices), 1))
    lanes = dot(owner, blocks.astype(BF16))
    keep = iota((rows, LANES), 1) % per == iota((rows, LANES), 0) % per
    return jnp.where(keep, lanes, 0.0).astype(BF16)


def field_rows(spreaded, per):
    pick = one(iota((8, LANES), 1) // per == iota((8, LANES), 0))
    return dot_nt(pick, spreaded)


def dispatch_kernel(devices, id_hbm, dest_hbm, gate_ref, tok_hbm, out_ref, meta_ref, *scratch):
    id_ref, dest_ref, tok_ref, sems = scratch
    rows = tok_ref.shape[0]
    per = rows // devices
    pairs = ((id_hbm, id_ref), (dest_hbm, dest_ref), (tok_hbm, tok_ref))
    copies = [pltpu.make_async_copy(*pair, sems.at[i]) for i, pair in enumerate(pairs)]
    for copy in copies:
        copy.start()
    copies[0].wait()
    copies[1].wait()
    ids = id_ref[...]
    dest = dest_ref[...]
    target = ids // 2
    local = ids - target * 2
    owner = dest // rows
    place = dest - owner * rows
    onehot = one(iota((devices, rows), 0) == target)
    counts = dot(onehot, earlier(rows))
    rank = jnp.sum(onehot.astype(F32) * counts, axis=0, keepdims=True).astype(I32)
    fields = [
        (local * DIGIT + place % DIGIT).astype(F32),
        (place // DIGIT).astype(F32),
        owner.astype(F32),
        gate_ref[...].astype(F32),
    ]
    meta_ref[...] = to_blocks(onehot, rank, fields, per)
    position = target * per + rank
    step = rows // 4
    copies[2].wait()
    for i in range(4):
        part = permute(position, rows, tok_ref[...], i * step, step)
        out_ref[i * step : (i + 1) * step, :] = part.astype(BF16)


def expert_kernel(
    devices, x_ref, meta_ref, gain_ref, in_ref, out_ref, y_ref, meta2_ref, xs, inputs, total, info, places, split
):
    rows, width = x_ref.shape
    per = rows // devices
    cap = inputs.shape[1]
    expert, chunk = pl.program_id(0), pl.program_id(1)

    @pl.when((expert == 0) & (chunk == 0))
    def _():
        spreaded = spread(meta_ref[...], rows, per)
        fields = field_rows(spreaded, per)
        code = fields[0:1].astype(I32)
        high = fields[1:2].astype(I32)
        owner = fields[2:3].astype(I32)
        local = code // DIGIT
        low = code - local * DIGIT
        onehot = one(iota((devices, rows), 0) == owner)
        is_local = jnp.where(local == 0, 1.0, 0.0)
        first = jnp.broadcast_to(is_local, (16, rows)).astype(BF16)
        counts = dot(jnp.concatenate([onehot, first], axis=0), earlier(rows))
        ranked = onehot.astype(F32) * counts[:devices]
        rank2 = jnp.sum(ranked, axis=0, keepdims=True).astype(I32)
        meta2_ref[...] = to_blocks(onehot, rank2, [low.astype(F32), high.astype(F32)], per)
        leave = owner * per + rank2
        before = counts[devices : devices + 1].astype(I32)
        number = jnp.sum(jnp.where(local == 0, 1.0, 0.0), axis=1, keepdims=True).astype(I32)
        position = jnp.where(local == 0, before, number + iota((1, rows), 1) - before)
        sort = one(iota((rows, rows), 0) == position)
        digit = iota((8, rows), 0)
        leave_digits = jnp.where(digit == 0, leave // DIGIT, leave % DIGIT).astype(F32)
        places[...] = dot_nt(leave_digits.astype(BF16), sort)
        put = one(iota((LANES, LANES), 0) // per == iota((LANES, LANES), 1))
        columns = dot(spreaded, put).astype(BF16)
        info[...] = dot(sort, columns)
        step = rows // 4
        for i in range(4):
            part = slice(i * step, (i + 1) * step)
            sorted_rows = dot(sort[part], x_ref[...]).astype(BF16)
            xs[part] = sorted_rows
            normed = rms_scale(sorted_rows, gain_ref[...])
            is_first = iota((step, 1), 0) + i * step < number
            none = jnp.zeros_like(normed)
            if (i + 1) * step <= cap:
                inputs[0, i * step : (i + 1) * step] = jnp.where(is_first, normed, none)
            if i * step >= rows - cap:
                low_row = i * step - (rows - cap)
                inputs[1, low_row : low_row + step] = jnp.where(is_first, none, normed)
        total[...] = jnp.zeros_like(total)
        split[0] = jnp.sum(jnp.where(local == 0, 1.0, 0.0)).astype(I32)

    tile = rows // 4
    own_rows = jnp.where(expert == 0, split[0], rows - split[0])
    for tiles in range(1, cap // tile + 1):
        size = tiles * tile

        @pl.when((own_rows <= size) & (own_rows > size - tile))
        def _():
            source = pl.multiple_of(expert * (cap - size), tile)
            base = pl.multiple_of(expert * (rows - size), tile)
            wide = dot(inputs[expert, pl.ds(source, size)], in_ref[0])
            hidden = jnp.maximum(wide, 0.0).astype(BF16)
            total[pl.ds(base, size), :] += dot(hidden, out_ref[0])

    @pl.when((expert == 1) & (chunk == pl.num_programs(1) - 1))
    def _():
        gate = info[:, 3:4]
        result = total[...].astype(BF16).astype(F32)
        xs[...] = (xs[...].astype(F32) + gate * result).astype(BF16)
        leave = (places[0:1] * DIGIT + places[1:2]).astype(I32)
        step = rows // 4
        for i in range(4):
            part = permute(leave, rows, xs[...], i * step, step)
            y_ref[i * step : (i + 1) * step, :] = part.astype(BF16)


def attention_kernel(devices, x_ref, meta_ref, gain_ref, qkv_ref, mix_ref, moe_ref, branch_ref, qkv, context):
    rows, width = x_ref.shape
    per = rows // devices
    seq = moe_ref.shape[0]
    fields = field_rows(spread(meta_ref[...], rows, per), per)
    place = (fields[1:2] * DIGIT + fields[0:1]).astype(I32)
    moved = permute(place, rows, x_ref[...], pl.program_id(0) * seq, seq).astype(BF16)
    moe_ref[...] = moved
    normed = rms_scale(moved, gain_ref[...])
    for i in range(3):
        part = slice(i * width, (i + 1) * width)
        qkv[:, part] = dot_nt(normed, qkv_ref[part]).astype(BF16)
    scale = 1.0 / HEAD_DIM**0.5
    left = iota((seq, LANES), 1) < HEAD_DIM
    ones = jnp.ones((seq, LANES), BF16)
    for pair in range(width // LANES):
        at = pair * LANES
        queries = qkv[:, at : at + LANES] * jnp.asarray(scale, BF16)
        keys = qkv[:, width + at : width + at + LANES]
        values = jnp.concatenate([qkv[:, 2 * width + at : 2 * width + at + LANES], ones], axis=1)
        halves = []
        for mask in (left, jnp.logical_not(left)):
            scores = dot_nt(jnp.where(mask, queries, jnp.zeros_like(queries)), keys)
            peak = jnp.max(scores, axis=1, keepdims=True)
            weights = jnp.exp(scores - peak).astype(BF16)
            mixed = dot(weights, values)
            halves.append(mixed[:, :LANES] / mixed[:, LANES:])
        context[:, at : at + LANES] = jnp.where(left, halves[0], halves[1]).astype(BF16)
    branch_ref[...] = dot_nt(context[...], mix_ref[...]).astype(BF16)


def peers(sizes):
    n_row, n_col = sizes
    devices = n_row * n_col
    row, col = lax.axis_index("row"), lax.axis_index("col")
    me = row * n_col + col

    def peer_of(i):
        return lax.rem(me + i, devices)

    def coords(device):
        return (device // n_col, lax.rem(device, n_col))

    return row, col, me, peer_of, coords


def greet_all(sizes):
    _, _, _, peer_of, coords = peers(sizes)
    barrier = pltpu.get_barrier_semaphore()

    def greet(i, carry):
        pl.semaphore_signal(
            barrier, inc=1, device_id=coords(peer_of(i)), device_id_type=pl.DeviceIdType.MESH
        )
        return carry

    lax.fori_loop(1, sizes[0] * sizes[1], greet, 0)
    return barrier


def remote(source, landing, send, recv, device):
    return pltpu.make_async_remote_copy(
        src_ref=source,
        dst_ref=landing,
        send_sem=send,
        recv_sem=recv,
        device_id=device,
        device_id_type=pl.DeviceIdType.MESH,
    )


def rows_exchange(sizes, x_ref, m_ref, y_ref, n_ref, send, recv, send_meta, recv_meta, own):
    devices = sizes[0] * sizes[1]
    per = x_ref.shape[0] // devices
    _, _, me, peer_of, coords = peers(sizes)

    def block(ref, device):
        return ref.at[pl.ds(pl.multiple_of(device * per, per), per)]

    def mine():
        return (
            pltpu.make_async_copy(block(x_ref, me), block(y_ref, me), own.at[0]),
            pltpu.make_async_copy(m_ref.at[me], n_ref.at[me], own.at[1]),
        )

    def copies(i, landing):
        peer = peer_of(i)
        target = coords(peer)
        return (
            remote(m_ref.at[peer], n_ref.at[landing], send_meta.at[i], recv_meta.at[i], target),
            remote(block(x_ref, peer), block(y_ref, landing), send.at[i], recv.at[i], target),
        )

    def start():
        def begin(i, carry):
            for copy in copies(i, me):
                copy.start()
            return carry

        for copy in mine():
            copy.start()
        lax.fori_loop(1, devices, begin, 0)

    def end():
        def finish(i, carry):
            for copy in copies(i, lax.rem(me + devices - i, devices)):
                copy.wait_send()
                copy.wait_recv()
            return carry

        for copy in mine():
            copy.wait()
        lax.fori_loop(1, devices, finish, 0)

    return start, end


def exchange1_kernel(sizes, x_ref, m_ref, w_ref, y_ref, n_ref, held_ref, *sems):
    chips = sizes[0] // 2
    row, col, _, _, _ = peers(sizes)
    chip, core = row // 2, lax.rem(row, 2)
    send_w, recv_w = sems[5:]
    start, end = rows_exchange(sizes, x_ref, m_ref, y_ref, n_ref, *sems[:5])
    barrier = greet_all(sizes)
    own = pltpu.make_async_copy(w_ref, held_ref.at[chip], send_w.at[0])
    own.start()
    pl.semaphore_wait(barrier, sizes[0] * sizes[1] - 1)
    start()

    def weights(i, landing):
        target = (lax.rem(chip + i, chips) * 2 + core, col)
        return remote(w_ref, held_ref.at[landing], send_w.at[i], recv_w.at[i], target)

    for i in range(1, chips):
        weights(i, chip).start()
    own.wait()
    for i in range(1, chips):
        weights(i, lax.rem(chip + chips - i, chips)).wait()
    end()


def exchange2_kernel(
    sizes, x_ref, m_ref, held_ref, mix_ref, y_ref, n_ref, wide_ref, full_ref, *sems
):
    n_row = sizes[0]
    chips, columns, _ = held_ref.shape
    mix_columns = mix_ref.shape[0]
    row, col, _, _, _ = peers(sizes)
    core = lax.rem(row, 2)
    local_w, send_w, recv_w, send_x, recv_x = sems[5:]
    start, end = rows_exchange(sizes, x_ref, m_ref, y_ref, n_ref, *sems[:5])
    barrier = greet_all(sizes)

    def part(ref, index, size):
        return ref.at[pl.ds(pl.multiple_of(index * size, size), size)]

    owned = [
        pltpu.make_async_copy(held_ref.at[c], part(wide_ref, 2 * c + core, columns), local_w.at[c])
        for c in range(chips)
    ]
    owned.append(pltpu.make_async_copy(mix_ref, part(full_ref, row, mix_columns), local_w.at[chips]))
    for copy in owned:
        copy.start()
    pl.semaphore_wait(barrier, sizes[0] * sizes[1] - 1)
    sibling = (row + 1 - 2 * core, col)

    def weights(c, side):
        landing = part(wide_ref, 2 * c + side, columns)
        return remote(held_ref.at[c], landing, send_w.at[c], recv_w.at[c], sibling)

    def mixing(i, landing):
        target = (lax.rem(row + i, n_row), col)
        landing = part(full_ref, landing, mix_columns)
        return remote(mix_ref, landing, send_x.at[i], recv_x.at[i], target)

    start()
    for c in range(chips):
        weights(c, core).start()
    for i in range(1, n_row):
        mixing(i, row).start()
    for copy in owned:
        copy.wait()
    for c in range(chips):
        weights(c, 1 - core).wait()
    for i in range(1, n_row):
        mixing(i, lax.rem(row + n_row - i, n_row)).wait()
    end()


def exchange_first(sizes, x, meta, qkv_weight, mix_weight):
    devices = sizes[0] * sizes[1]
    rows, width = x.shape
    meta = meta.reshape(devices, 1, LANES)
    if rows // devices % 16 or sizes[0] % 2:
        held = (
            lax.all_gather(qkv_weight, "row", axis=0, tiled=True),
            lax.all_gather(mix_weight, "row", axis=0, tiled=True),
        )
        return *all_to_all(devices, x, meta), held
    vmem = pl.BlockSpec()
    hbm = pl.BlockSpec(memory_space=pl.ANY)
    chips = sizes[0] // 2
    y, n, held = pl.pallas_call(
        functools.partial(exchange1_kernel, sizes),
        out_shape=(
            jax.ShapeDtypeStruct(x.shape, x.dtype),
            jax.ShapeDtypeStruct(meta.shape, meta.dtype),
            jax.ShapeDtypeStruct((chips, *qkv_weight.shape), BF16),
        ),
        in_specs=[vmem, vmem, hbm],
        out_specs=(vmem, vmem, hbm),
        scratch_shapes=[pltpu.SemaphoreType.DMA((devices,))] * 4
        + [pltpu.SemaphoreType.DMA((2,))]
        + [pltpu.SemaphoreType.DMA((chips,))] * 2,
        compiler_params=pltpu.CompilerParams(
            collective_id=1, has_side_effects=True, vmem_limit_bytes=32 * MIB
        ),
        name="exchange1",
    )(x, meta, qkv_weight)
    return y, n.reshape(devices, LANES), held


def all_to_all(devices, x, meta):
    rows, width = x.shape
    y, n = (
        lax.all_to_all(part, ("row", "col"), split_axis=0, concat_axis=0, tiled=True)
        for part in (x.reshape(devices, rows // devices, width), meta)
    )
    return y.reshape(rows, width), n.reshape(devices, LANES)


def exchange_second(sizes, x, meta, held, mix_weight):
    devices = sizes[0] * sizes[1]
    rows, width = x.shape
    meta = meta.reshape(devices, 1, LANES)
    if rows // devices % 16 or sizes[0] % 2:
        return *all_to_all(devices, x, meta), *held
    vmem = pl.BlockSpec()
    hbm = pl.BlockSpec(memory_space=pl.ANY)
    n_row = sizes[0]
    chips, columns, depth = held.shape
    y, n, wide, full = pl.pallas_call(
        functools.partial(exchange2_kernel, sizes),
        out_shape=(
            jax.ShapeDtypeStruct(x.shape, x.dtype),
            jax.ShapeDtypeStruct(meta.shape, meta.dtype),
            jax.ShapeDtypeStruct((n_row * columns, depth), BF16),
            jax.ShapeDtypeStruct((n_row * mix_weight.shape[0], depth), BF16),
        ),
        in_specs=[vmem, vmem, hbm, hbm],
        out_specs=(vmem,) * 4,
        scratch_shapes=[pltpu.SemaphoreType.DMA((devices,))] * 4
        + [pltpu.SemaphoreType.DMA((2,))]
        + [pltpu.SemaphoreType.DMA((chips + 1,))]
        + [pltpu.SemaphoreType.DMA((chips,))] * 2
        + [pltpu.SemaphoreType.DMA((n_row,))] * 2,
        compiler_params=pltpu.CompilerParams(
            collective_id=2, has_side_effects=True, vmem_limit_bytes=40 * MIB
        ),
        name="exchange2",
    )(x, meta, held, mix_weight)
    return y, n.reshape(devices, LANES), wide, full


def whole(shape):
    return pl.BlockSpec(shape, lambda *_: (0,) * len(shape))


def shards(
    sizes,
    tokens,
    gate_prob,
    expert_id,
    dest_row,
    ff_gain,
    expert_in,
    expert_out,
    attn_gain,
    qkv_weight,
    mix_weight,
):
    rows, width = tokens.shape
    devices = sizes[0] * sizes[1]
    hidden = expert_in.shape[2]
    cap = rows * 3 // 4
    meta_shape = jax.ShapeDtypeStruct((devices, LANES), F32)
    qkv_weight, mix_weight = qkv_weight.T, mix_weight.T
    rows_shape = jax.ShapeDtypeStruct((rows, width), BF16)

    leaving, meta = pl.pallas_call(
        functools.partial(dispatch_kernel, devices),
        out_shape=(rows_shape, meta_shape),
        in_specs=[
            pl.BlockSpec(memory_space=pl.ANY),
            pl.BlockSpec(memory_space=pl.ANY),
            pl.BlockSpec(),
            pl.BlockSpec(memory_space=pl.ANY),
        ],
        scratch_shapes=[
            pltpu.VMEM((1, rows), I32),
            pltpu.VMEM((1, rows), I32),
            pltpu.VMEM((rows, width), BF16),
            pltpu.SemaphoreType.DMA((3,)),
        ],
        compiler_params=pltpu.CompilerParams(vmem_limit_bytes=32 * MIB),
        name="dispatch",
    )(
        expert_id.reshape(1, rows),
        dest_row.reshape(1, rows),
        gate_prob.reshape(1, rows),
        tokens,
    )
    arrived, meta, held = exchange_first(sizes, leaving, meta, qkv_weight, mix_weight)

    chunk = hidden // 4
    leaving, meta = pl.pallas_call(
        functools.partial(expert_kernel, devices),
        out_shape=(rows_shape, meta_shape),
        grid=(2, hidden // chunk),
        in_specs=[
            whole((rows, width)),
            whole((devices, LANES)),
            whole((1, width)),
            pl.BlockSpec((1, width, chunk), lambda e, c: (e, 0, c)),
            pl.BlockSpec((1, chunk, width), lambda e, c: (e, c, 0)),
        ],
        out_specs=(whole((rows, width)), whole((devices, LANES))),
        scratch_shapes=[
            pltpu.VMEM((rows, width), BF16),
            pltpu.VMEM((2, cap, width), BF16),
            pltpu.VMEM((rows, width), F32),
            pltpu.VMEM((rows, LANES), F32),
            pltpu.VMEM((8, rows), F32),
            pltpu.SMEM((1,), I32),
        ],
        compiler_params=pltpu.CompilerParams(vmem_limit_bytes=48 * MIB),
        name="experts",
    )(arrived, meta, ff_gain.reshape(1, width), expert_in, expert_out)
    arrived, meta, qkv_full, mix_full = exchange_second(sizes, leaving, meta, held, mix_weight)

    return pl.pallas_call(
        functools.partial(attention_kernel, devices),
        out_shape=(rows_shape, rows_shape),
        grid=(rows // SEQ,),
        in_specs=[
            whole((rows, width)),
            whole((devices, LANES)),
            whole((1, width)),
            whole((3 * width, width)),
            whole((width, width)),
        ],
        out_specs=(
            pl.BlockSpec((SEQ, width), lambda s: (s, 0)),
            pl.BlockSpec((SEQ, width), lambda s: (s, 0)),
        ),
        scratch_shapes=[
            pltpu.VMEM((SEQ, 3 * width), BF16),
            pltpu.VMEM((SEQ, width), BF16),
        ],
        compiler_params=pltpu.CompilerParams(vmem_limit_bytes=32 * MIB),
        name="attention",
    )(arrived, meta, attn_gain.reshape(1, width), qkv_full, mix_full)


def solution(mesh):
    placed = (
        P(("row", "col"), None),
        P(("row", "col")),
        P(("row", "col")),
        P(("row", "col")),
        P(),
        P(("row", "col"), None, None),
        P(("row", "col"), None, None),
        P(),
        P(None, "row"),
        P(None, "row"),
    )
    sizes = (mesh.shape["row"], mesh.shape["col"])
    return jax.shard_map(
        functools.partial(shards, sizes),
        mesh=mesh,
        in_specs=placed,
        out_specs=(P(("row", "col"), None), P(("row", "col"), None)),
        check_vma=False,
    )
```
